32 devices in a mesh: branch: 4 (over y, x), row: 8 (over z, core).
Axes of the slice: x: 2, y: 2, z: 4, core: 2. Of those that a mesh axis runs over, the one named last changes fastest.
Arguments:
- root_cov: bfloat16 [2304, 2304], P('row', 'branch')
- diag_factor: float32 [4, 3, 576, 576], P('branch')
- panel_factor: float32 [4, 3, 2304, 576], P('branch', None, 'row'), may hold values from -0.009765625 to 0.009765625
- chain_factor: float32 [4, 2, 576, 576], P('branch'), may hold values from -0.25 to 0.25
- panel_tiles: int32 [4, 3], P('branch'), may hold values from 0 to 3, as said below
Outputs:
- panel_cov: float32 [4, 3, 2304, 576], P('branch', None, 'row')
- block_cov: float32 [4, 5, 576, 576], P('branch')
The draws below stay inside these ranges and needn't reach their ends.
Inputs may be any that keep to these rules, and one draw needn't show every extreme that they name: `panel_tiles`: the entries of a row are distinct; the first 2 and the first 1 entries of a row are the level-two and level-three patterns.
All inputs are finite; a program needn't handle non-finite values.
Results may differ from the reference program's by a relative error of at most 0.0029.
Values may be sent and summed in bfloat16 or wider, within the bound.
A program may use at most 192 MiB of HBM per device.

```python
import math
import jax
import jax.numpy as jnp
from jax import lax

W = 576
RT = 4
NR = 2304
K1 = 3
K2 = 2
K3 = 1
N_BRANCH = 4


def draw_root_cov(key, part):
    noise = jax.random.normal(key, (NR, NR), jnp.float32)
    spread = jax.random.uniform(jax.random.fold_in(key, 7), (NR,), jnp.float32, 1.0, 2.0)
    offdiag = (noise + noise.T) * (0.5 / math.sqrt(2.0 * NR))
    return (W * (offdiag + jnp.diag(spread))).astype(jnp.bfloat16)


def draw_diag_factor(key, part):
    noise = jax.random.normal(key, (N_BRANCH, 3, W, W), jnp.float32)
    spread = jax.random.uniform(jax.random.fold_in(key, 11), (N_BRANCH, 3, W, 1), jnp.float32, 1.0, 2.0)
    lower = jnp.tril(noise, -1) * (0.5 / math.sqrt(1.0 * W))
    identity = jnp.eye(W, dtype=jnp.float32)
    return lower + identity * spread


def draw_panel_tiles(key, part):
    keys = jax.random.split(key, N_BRANCH)
    orders = jax.vmap(lambda single: jax.random.permutation(single, RT))(keys)
    return orders[:, :K1].astype(jnp.int32)


def level_of(own_key, extent, pieces, least, largest):
    factor_of, own = 1.0, jax.random.fold_in(own_key, 6)
    for dim, shards_of in pieces:
        steps = jnp.exp(jax.random.uniform(jax.random.fold_in(own, dim), (shards_of,), jnp.float32, least / len(pieces), largest / len(pieces)))
        factor_of = factor_of * jnp.repeat(steps, extent[dim] // shards_of).reshape([-1 if axis == dim else 1 for axis in range(len(extent))])
    return factor_of


def normal_values(rng, dims, deviation, reach, shards=(), kind=jnp.bfloat16):
    level = level_of(rng, dims, shards, -0.22, 0.18) if shards else 1.0
    values = jax.random.normal(rng, dims, jnp.float32) * deviation * level
    return jnp.minimum(jnp.maximum(values, -reach), reach).astype(kind)


def setup_inputs(seed: int = 0) -> dict:
    splits = jax.random.split(jax.random.key(seed), 6)
    return {
        "root_cov": draw_root_cov(jax.random.fold_in(splits[5], 71), 0),
        "diag_factor": draw_diag_factor(jax.random.fold_in(splits[5], 71), 0),
        "panel_factor": normal_values(splits[2], (N_BRANCH, 3, NR, W), (W * W) ** -0.5, 0.009765625, ((0, 4), (2, 8)), jnp.float32),
        "chain_factor": normal_values(splits[3], (N_BRANCH, 2, W, W), W ** -0.5, 0.25, ((0, 4),), jnp.float32),
        "panel_tiles": draw_panel_tiles(jax.random.fold_in(splits[5], 71), 0),
    }


HIGHEST = lax.Precision.HIGHEST

def product(left_mat, right_mat):
    return jnp.dot(left_mat.astype(jnp.float32), right_mat.astype(jnp.float32), precision=HIGHEST, preferred_element_type=jnp.float32)

def reference(root_cov, diag_factor, panel_factor, chain_factor, panel_tiles):
    identity = jnp.eye(W, dtype=jnp.float32)
    tile_of_row = (jnp.arange(NR) // W).astype(jnp.int32)
    root_wide = root_cov.astype(jnp.float32)
    counts = (K1, K2, K3)
    panels = [[] for branch_index in range(N_BRANCH)]
    blocks = [[] for branch_index in range(N_BRANCH)]
    crosses = [[] for branch_index in range(N_BRANCH)]
    for layer_index in range(3):
        inverses = []
        chosen_all = []
        scaled_all = []
        for branch_index in range(N_BRANCH):
            inverse = jax.scipy.linalg.solve_triangular(diag_factor[branch_index, layer_index], identity, lower=True)
            chosen = jnp.any(tile_of_row[:, None] == panel_tiles[branch_index, :counts[layer_index]][None, :], axis=1)
            scaled = jnp.where(chosen[:, None], product(panel_factor[branch_index, layer_index], inverse), 0.0)
            inverses.append(inverse)
            chosen_all.append(chosen)
            scaled_all.append(scaled)
        rounded = jnp.concatenate([lax.optimization_barrier(item.astype(jnp.bfloat16)).astype(jnp.float32) for item in scaled_all], axis=1)
        projected = product(root_wide, rounded)
        for branch_index in range(N_BRANCH):
            inverse = inverses[branch_index]
            gram = product(inverse.T, inverse)
            chosen = chosen_all[branch_index]
            scaled = scaled_all[branch_index]
            gathered = projected[:, branch_index * W:(branch_index + 1) * W]
            if layer_index == 0:
                panel = -jnp.where(chosen[:, None], gathered, 0.0)
                block = gram - product(scaled.T, panel)
            else:
                previous_panel = panels[branch_index][-1]
                previous_block = blocks[branch_index][-1]
                scaled_chain = product(chain_factor[branch_index, layer_index - 1], inverse)
                panel = -jnp.where(chosen[:, None], gathered + product(previous_panel, scaled_chain), 0.0)
                cross = -(product(previous_panel.T, scaled) + product(previous_block, scaled_chain))
                block = gram - product(scaled.T, panel) - product(scaled_chain.T, cross)
                crosses[branch_index].append(cross)
            panels[branch_index].append(panel)
            blocks[branch_index].append(block)
    panel_cov = jnp.stack([jnp.stack(panels[branch_index]) for branch_index in range(N_BRANCH)])
    block_cov = jnp.stack([jnp.stack(blocks[branch_index] + crosses[branch_index]) for branch_index in range(N_BRANCH)])
    return (panel_cov, block_cov)
```

```python
import functools
import jax
import jax.numpy as jnp
from jax import lax
from jax.experimental import pallas as pl
from jax.experimental.pallas import tpu as pltpu
from jax.sharding import PartitionSpec as P

BF = jnp.bfloat16
F32 = jnp.float32


def product(left_mat, right_mat):
    return jnp.dot(left_mat, right_mat, precision=lax.Precision.HIGH, preferred_element_type=F32)


def split(x):
    hi = x.astype(BF)
    return hi, (x - hi.astype(F32)).astype(BF)


def mm(a, b):
    return jnp.dot(a, b, preferred_element_type=F32)


def dot3(a, b):
    a_hi, a_lo = a
    b_hi, b_lo = b
    return mm(a_hi, b_hi) + (mm(a_lo, b_hi) + mm(a_hi, b_lo))


def inverse_kernel(size, window, l_ref, out_ref):
    count = size // window
    row = lax.broadcasted_iota(jnp.int32, (window, window), 0)
    col = lax.broadcasted_iota(jnp.int32, (window, window), 1)
    eye = row == col
    diagonals = []
    for w in range(count):
        at = slice(w * window, (w + 1) * window)
        block = l_ref[0, 0, at, at]
        kept = jnp.where(eye, block, 0.0)
        down = 1.0 / jnp.sum(kept, axis=1, keepdims=True)
        across = 1.0 / jnp.sum(kept, axis=0, keepdims=True)
        diagonals.append((block * down, across))
    found = []
    for scaled, across in diagonals:
        x = jnp.where(eye, 1.0, 0.0)
        x = x - jnp.where((row // 2 == col // 2) & (row > col), scaled, 0.0)
        found.append(x)
    k = 2
    while k < window:
        pair = (row // (2 * k) == col // (2 * k)) & (row // k > col // k)
        for w in range(count):
            x = found[w]
            parts = split(x)
            right = dot3(split(jnp.where(pair, diagonals[w][0], 0.0)), parts)
            found[w] = x - dot3(parts, split(right))
        k *= 2
    found = [x * diagonals[w][1] for w, x in enumerate(found)]
    done = {}
    for w in range(count):
        done[w, w] = split(found[w])
        out_ref[0, w * window:(w + 1) * window, w * window:(w + 1) * window] = found[w]
    for gap in range(1, count):
        for c in range(count - gap):
            r = c + gap
            total = None
            for m in range(c, r):
                below = split(l_ref[0, 0, r * window:(r + 1) * window, m * window:(m + 1) * window])
                term = dot3(below, done[m, c])
                total = term if total is None else total + term
            value = -dot3(done[r, r], split(total))
            done[r, c] = split(value)
            out_ref[0, r * window:(r + 1) * window, c * window:(c + 1) * window] = value
            out_ref[0, c * window:(c + 1) * window, r * window:(r + 1) * window] = jnp.zeros(
                (window, window), F32
            )


def inverses(diag_factor):
    levels, size = diag_factor.shape[1], diag_factor.shape[-1]
    return pl.pallas_call(
        functools.partial(inverse_kernel, size, size // 3),
        grid=(levels,),
        in_specs=[pl.BlockSpec((1, 1, size, size), lambda i: (0, i, 0, 0))],
        out_specs=pl.BlockSpec((1, size, size), lambda i: (i, 0, 0)),
        out_shape=jax.ShapeDtypeStruct((levels, size, size), F32),
        compiler_params=pltpu.CompilerParams(vmem_limit_bytes=48 * 2**20),
        name="inverses",
    )(diag_factor)


def on_device(root_cov, diag_factor, panel_factor, chain_factor, panel_tiles):
    node_width = diag_factor.shape[-1]
    rows_here = panel_factor.shape[2]
    per_tile = node_width // rows_here
    row_count = lax.axis_size("row")
    tile_total = row_count // per_tile
    counts = (3 * tile_total // 4, tile_total // 2, tile_total // 4)
    root_rows = lax.all_gather(root_cov, "branch", axis=1, tiled=True)
    me = lax.axis_index("row")
    my_tile = me // per_tile
    inverse_all = inverses(diag_factor)
    share = -(-node_width // row_count // 8) * 8
    padded = jnp.pad(inverse_all, ((0, 0), (0, share * row_count - node_width), (0, 0)))
    mine = lax.dynamic_slice_in_dim(padded, me * share, share, axis=1)
    chosen = [jnp.any(panel_tiles[0, : counts[i]] == my_tile) for i in range(3)]
    scaled = [
        jnp.where(chosen[i], product(panel_factor[0, i], inverse_all[i]), 0.0) for i in range(3)
    ]
    panels = []
    blocks = []
    crosses = []
    for i in range(3):
        gathered = jnp.dot(
            root_rows,
            lax.all_gather(scaled[i].astype(BF), "row", axis=0, tiled=True),
            preferred_element_type=F32,
        )
        left = jnp.concatenate([mine[i], scaled[i]], axis=0)
        if i == 0:
            panel = -jnp.where(chosen[i], gathered, 0.0)
            block = product(left.T, jnp.concatenate([mine[i], -panel], axis=0))
        else:
            chain = product(chain_factor[0, i - 1], inverse_all[i])
            panel = -jnp.where(chosen[i], gathered + product(panels[-1], chain), 0.0)
            cross = -(product(panels[-1].T, scaled[i]) + product(blocks[-1], chain))
            block = product(left.T, jnp.concatenate([mine[i], -panel], axis=0)) - product(
                chain.T, cross
            )
            crosses.append(cross)
        panels.append(panel)
        blocks.append(block)
    total = lax.psum(jnp.stack(blocks + crosses), "row")
    return (jnp.stack(panels)[None], total[None])


def solution(mesh):
    in_specs = (
        P("row", "branch"),
        P("branch", None, None, None),
        P("branch", None, "row", None),
        P("branch", None, None, None),
        P("branch", None),
    )
    out_specs = (P("branch", None, "row", None), P("branch", None, None, None))
    return jax.shard_map(
        on_device, mesh=mesh, in_specs=in_specs, out_specs=out_specs, check_vma=False
    )
```

```python
import functools
import jax
import jax.numpy as jnp
from jax import lax
from jax.experimental import pallas as pl
from jax.experimental.pallas import tpu as pltpu
from jax.sharding import PartitionSpec as P

BF = jnp.bfloat16
F32 = jnp.float32
MESH = pl.DeviceIdType.MESH


def product(left_mat, right_mat):
    return jnp.dot(left_mat, right_mat, precision=lax.Precision.HIGH, preferred_element_type=F32)


def split(x):
    hi = x.astype(BF)
    return hi, (x - hi.astype(F32)).astype(BF)


def mm(a, b):
    return jnp.dot(a, b, preferred_element_type=F32)


def dot3(a, b):
    a_hi, a_lo = a
    b_hi, b_lo = b
    return mm(a_hi, b_hi) + (mm(a_lo, b_hi) + mm(a_hi, b_lo))


def inverse_kernel(size, window, l_ref, out_ref):
    count = size // window
    row = lax.broadcasted_iota(jnp.int32, (window, window), 0)
    col = lax.broadcasted_iota(jnp.int32, (window, window), 1)
    eye = row == col
    diagonals = []
    for w in range(count):
        at = slice(w * window, (w + 1) * window)
        block = l_ref[0, 0, at, at]
        kept = jnp.where(eye, block, 0.0)
        down = 1.0 / jnp.sum(kept, axis=1, keepdims=True)
        across = 1.0 / jnp.sum(kept, axis=0, keepdims=True)
        diagonals.append((block * down, across))
    found = []
    for scaled, across in diagonals:
        x = jnp.where(eye, 1.0, 0.0)
        x = x - jnp.where((row // 2 == col // 2) & (row > col), scaled, 0.0)
        found.append(x)
    k = 2
    while k < window:
        pair = (row // (2 * k) == col // (2 * k)) & (row // k > col // k)
        for w in range(count):
            x = found[w]
            parts = split(x)
            right = dot3(split(jnp.where(pair, diagonals[w][0], 0.0)), parts)
            found[w] = x - dot3(parts, split(right))
        k *= 2
    found = [x * diagonals[w][1] for w, x in enumerate(found)]
    done = {}
    for w in range(count):
        done[w, w] = split(found[w])
        out_ref[0, w * window:(w + 1) * window, w * window:(w + 1) * window] = found[w]
    for gap in range(1, count):
        for c in range(count - gap):
            r = c + gap
            total = None
            for m in range(c, r):
                below = split(l_ref[0, 0, r * window:(r + 1) * window, m * window:(m + 1) * window])
                term = dot3(below, done[m, c])
                total = term if total is None else total + term
            value = -dot3(done[r, r], split(total))
            done[r, c] = split(value)
            out_ref[0, r * window:(r + 1) * window, c * window:(c + 1) * window] = value
            out_ref[0, c * window:(c + 1) * window, r * window:(r + 1) * window] = jnp.zeros(
                (window, window), F32
            )


def inverses(diag_factor):
    levels, size = diag_factor.shape[1], diag_factor.shape[-1]
    return pl.pallas_call(
        functools.partial(inverse_kernel, size, size // 3),
        grid=(levels,),
        in_specs=[pl.BlockSpec((1, 1, size, size), lambda i: (0, i, 0, 0))],
        out_specs=pl.BlockSpec((1, size, size), lambda i: (i, 0, 0)),
        out_shape=jax.ShapeDtypeStruct((levels, size, size), F32),
        compiler_params=pltpu.CompilerParams(vmem_limit_bytes=48 * 2**20),
        name="inverses",
    )(diag_factor)


def sum_kernel(x_ref, out_ref, pair, send, landed, right_got, left_got, right_sib, left_sib, final,
               final_sib, pair_s, pair_r, rs_s, rs_r, right_s, right_r, left_s, left_r, sib_s, sib_r):
    me = lax.axis_index("row")
    z = me // 2
    core = me % 2
    sibling = 2 * z + 1 - core

    def at_chip(chip):
        return {"row": 2 * chip + core}

    barrier = pltpu.get_barrier_semaphore()
    pl.semaphore_signal(barrier, inc=1, device_id={"row": sibling}, device_id_type=MESH)
    for k in (1, 2, 3):
        pl.semaphore_signal(
            barrier, inc=1, device_id=at_chip((z + k) % 4), device_id_type=MESH
        )
    pl.semaphore_wait(barrier, 4)

    def copy(src, dst, send_sem, recv_sem, target):
        return pltpu.make_async_remote_copy(
            src_ref=src, dst_ref=dst, send_sem=send_sem, recv_sem=recv_sem,
            device_id=target, device_id_type=MESH,
        )

    to_pair = {}
    for k in (2, 1, 3, 0):
        to_pair[k] = copy(
            x_ref.at[1 - core, (z + k) % 4], pair.at[k], pair_s.at[k], pair_r.at[k],
            {"row": sibling},
        )
        to_pair[k].start()
    scatter = {}
    for k in (2, 1, 3):
        to_pair[k].wait_recv()
        send[k - 1] = (x_ref[core, (z + k) % 4] + pair[k]).astype(BF)
        scatter[k] = copy(
            send.at[k - 1], landed.at[k - 1], rs_s.at[k - 1], rs_r.at[k - 1],
            at_chip((z + k) % 4),
        )
        scatter[k].start()
    to_pair[0].wait_recv()
    pair[0] = pair[0] + x_ref[core, z]
    for k in (1, 3, 2):
        scatter[k].wait_recv()
        pair[0] = pair[0] + landed[k - 1].astype(F32)
    final[...] = pair[0].astype(BF)

    rights, lefts, sibs = {}, {}, {}
    sibs[0] = copy(final, final_sib, sib_s.at[0], sib_r.at[0], {"row": sibling})
    for s in (1, 2, 3):
        rights[s] = copy(
            final if s == 1 else right_got.at[s - 2], right_got.at[s - 1],
            right_s.at[s - 1], right_r.at[s - 1], at_chip(jnp.minimum(z + 1, 3)),
        )
        lefts[s] = copy(
            final if s == 1 else left_got.at[s - 2], left_got.at[s - 1],
            left_s.at[s - 1], left_r.at[s - 1], at_chip(jnp.maximum(z - 1, 0)),
        )
        sibs[s] = copy(
            right_got.at[s - 1], right_sib.at[s - 1], sib_s.at[s], sib_r.at[s], {"row": sibling}
        )
        sibs[-s] = copy(
            left_got.at[s - 1], left_sib.at[s - 1], sib_s.at[3 + s], sib_r.at[3 + s],
            {"row": sibling},
        )

    def goes_right(s):
        return (z < 3) & (z >= s - 1)

    def goes_left(s):
        return (z > 0) & (z + s <= 4)

    pl.when(goes_right(1))(rights[1].start)
    pl.when(goes_left(1))(lefts[1].start)
    sibs[0].start()
    out_ref[core, z] = final[...].astype(F32)
    for s in (1, 2, 3):
        @pl.when(z >= s)
        def _():
            rights[s].wait_recv()
            sibs[s].start()

        if s < 3:
            pl.when(goes_right(s + 1))(rights[s + 1].start)

        @pl.when(z + s <= 3)
        def _():
            lefts[s].wait_recv()
            sibs[-s].start()

        if s < 3:
            pl.when(goes_left(s + 1))(lefts[s + 1].start)

        @pl.when(z >= s)
        def _():
            out_ref[core, z - s] = right_got[s - 1].astype(F32)

        @pl.when(z + s <= 3)
        def _():
            out_ref[core, z + s] = left_got[s - 1].astype(F32)

    sibs[0].wait_recv()
    out_ref[1 - core, z] = final_sib[...].astype(F32)
    for s in (1, 2, 3):
        @pl.when(z >= s)
        def _():
            sibs[s].wait_recv()
            out_ref[1 - core, z - s] = right_sib[s - 1].astype(F32)

        @pl.when(z + s <= 3)
        def _():
            sibs[-s].wait_recv()
            out_ref[1 - core, z + s] = left_sib[s - 1].astype(F32)

    for k in (0, 1, 2, 3):
        to_pair[k].wait_send()
        if k:
            scatter[k].wait_send()
    sibs[0].wait_send()
    for s in (1, 2, 3):
        pl.when(goes_right(s))(rights[s].wait_send)
        pl.when(goes_left(s))(lefts[s].wait_send)
        pl.when(z >= s)(sibs[s].wait_send)
        pl.when(z + s <= 3)(sibs[-s].wait_send)


def line_sum(parts):
    total = sum(p.shape[0] for p in parts)
    columns = parts[0].shape[1]
    rows = -(-total // 128) * 16
    x = jnp.concatenate(parts + [jnp.zeros((8 * rows - total, columns), F32)], axis=0)
    dma = pltpu.SemaphoreType.DMA
    whole = pl.BlockSpec(memory_space=pltpu.VMEM)
    out = pl.pallas_call(
        sum_kernel,
        out_shape=jax.ShapeDtypeStruct((2, 4, rows, columns), F32),
        in_specs=[whole],
        out_specs=whole,
        scratch_shapes=[
            pltpu.VMEM((4, rows, columns), F32),
            *[pltpu.VMEM((3, rows, columns), BF) for _ in range(6)],
            pltpu.VMEM((rows, columns), BF),
            pltpu.VMEM((rows, columns), BF),
            dma((4,)), dma((4,)),
            *[dma((3,)) for _ in range(6)],
            dma((7,)), dma((7,)),
        ],
        compiler_params=pltpu.CompilerParams(
            collective_id=0, has_side_effects=True, vmem_limit_bytes=48 * 2**20
        ),
        name="line_sum",
    )(x.reshape(2, 4, rows, columns))
    return out.reshape(8 * rows, columns)[:total]


def on_device(root_cov, diag_factor, panel_factor, chain_factor, panel_tiles):
    node_width = diag_factor.shape[-1]
    rows_here = panel_factor.shape[2]
    per_tile = node_width // rows_here
    row_count = lax.axis_size("row")
    tile_total = row_count // per_tile
    counts = (3 * tile_total // 4, tile_total // 2, tile_total // 4)
    root_rows = lax.all_gather(root_cov, "branch", axis=1, tiled=True)
    me = lax.axis_index("row")
    my_tile = me // per_tile
    inverse_all = inverses(diag_factor)
    share = -(-node_width // row_count // 8) * 8
    padded = jnp.pad(inverse_all, ((0, 0), (0, share * row_count - node_width), (0, 0)))
    mine = lax.dynamic_slice_in_dim(padded, me * share, share, axis=1)
    chosen = [jnp.any(panel_tiles[0, : counts[i]] == my_tile) for i in range(3)]
    scaled = [
        jnp.where(chosen[i], product(panel_factor[0, i], inverse_all[i]), 0.0) for i in range(3)
    ]
    panels = []
    blocks = []
    crosses = []
    for i in range(3):
        rounded = scaled[i].astype(BF)
        if counts[i] == 1 and per_tile == 2:
            sibling = me + 1 - 2 * (me % 2)
            theirs = lax.ppermute(rounded, "row", [(d, d ^ 1) for d in range(row_count)])
            gathered = jnp.dot(
                lax.dynamic_slice_in_dim(root_rows, me * rows_here, rows_here, axis=1),
                rounded,
                preferred_element_type=F32,
            ) + jnp.dot(
                lax.dynamic_slice_in_dim(root_rows, sibling * rows_here, rows_here, axis=1),
                theirs,
                preferred_element_type=F32,
            )
        else:
            gathered = jnp.dot(
                root_rows,
                lax.all_gather(rounded, "row", axis=0, tiled=True),
                preferred_element_type=F32,
            )
        left = jnp.concatenate([mine[i], scaled[i]], axis=0)
        if i == 0:
            panel = -jnp.where(chosen[i], gathered, 0.0)
            block = product(left.T, jnp.concatenate([mine[i], -panel], axis=0))
        else:
            chain = product(chain_factor[0, i - 1], inverse_all[i])
            panel = -jnp.where(chosen[i], gathered + product(panels[-1], chain), 0.0)
            cross = -(product(panels[-1].T, scaled[i]) + product(blocks[-1], chain))
            block = product(left.T, jnp.concatenate([mine[i], -panel], axis=0)) - product(
                chain.T, cross
            )
            crosses.append(cross)
        panels.append(panel)
        blocks.append(block)
    parts = blocks + crosses
    if row_count == 8:
        total = line_sum(parts).reshape(len(parts), node_width, node_width)
    else:
        total = lax.psum(jnp.stack(parts), "row")
    return (jnp.stack(panels)[None], total[None])


def solution(mesh):
    in_specs = (
        P("row", "branch"),
        P("branch", None, None, None),
        P("branch", None, "row", None),
        P("branch", None, None, None),
        P("branch", None),
    )
    out_specs = (P("branch", None, "row", None), P("branch", None, None, None))
    return jax.shard_map(
        on_device, mesh=mesh, in_specs=in_specs, out_specs=out_specs, check_vma=False
    )
```

```python
import functools
import jax
import jax.numpy as jnp
from jax import lax
from jax.experimental import pallas as pl
from jax.experimental.pallas import tpu as pltpu
from jax.sharding import PartitionSpec as P

BF = jnp.bfloat16
F32 = jnp.float32
MESH = pl.DeviceIdType.MESH


def product(left_mat, right_mat):
    return jnp.dot(left_mat, right_mat, precision=lax.Precision.HIGH, preferred_element_type=F32)


def split(x):
    hi = x.astype(BF)
    return hi, (x - hi.astype(F32)).astype(BF)


def mm(a, b):
    return jnp.dot(a, b, preferred_element_type=F32)


def dot3(a, b):
    a_hi, a_lo = a
    b_hi, b_lo = b
    return mm(a_hi, b_hi) + (mm(a_lo, b_hi) + mm(a_hi, b_lo))


def inverse_kernel(size, window, l_ref, out_ref):
    count = size // window
    row = lax.broadcasted_iota(jnp.int32, (window, window), 0)
    col = lax.broadcasted_iota(jnp.int32, (window, window), 1)
    eye = row == col
    diagonals = []
    for w in range(count):
        at = slice(w * window, (w + 1) * window)
        block = l_ref[0, 0, at, at]
        kept = jnp.where(eye, block, 0.0)
        down = 1.0 / jnp.sum(kept, axis=1, keepdims=True)
        across = 1.0 / jnp.sum(kept, axis=0, keepdims=True)
        diagonals.append((block * down, across))
    found = []
    for scaled, across in diagonals:
        x = jnp.where(eye, 1.0, 0.0)
        x = x - jnp.where((row // 2 == col // 2) & (row > col), scaled, 0.0)
        found.append(x)
    k = 2
    while k < window:
        pair = (row // (2 * k) == col // (2 * k)) & (row // k > col // k)
        for w in range(count):
            x = found[w]
            parts = split(x)
            right = dot3(split(jnp.where(pair, diagonals[w][0], 0.0)), parts)
            found[w] = x - dot3(parts, split(right))
        k *= 2
    found = [x * diagonals[w][1] for w, x in enumerate(found)]
    done = {}
    for w in range(count):
        done[w, w] = split(found[w])
        out_ref[0, w * window:(w + 1) * window, w * window:(w + 1) * window] = found[w]
    for gap in range(1, count):
        for c in range(count - gap):
            r = c + gap
            total = None
            for m in range(c, r):
                below = split(l_ref[0, 0, r * window:(r + 1) * window, m * window:(m + 1) * window])
                term = dot3(below, done[m, c])
                total = term if total is None else total + term
            value = -dot3(done[r, r], split(total))
            done[r, c] = split(value)
            out_ref[0, r * window:(r + 1) * window, c * window:(c + 1) * window] = value
            out_ref[0, c * window:(c + 1) * window, r * window:(r + 1) * window] = jnp.zeros(
                (window, window), F32
            )


def inverses(diag_factor):
    levels, size = diag_factor.shape[1], diag_factor.shape[-1]
    return pl.pallas_call(
        functools.partial(inverse_kernel, size, size // 3),
        grid=(levels,),
        in_specs=[pl.BlockSpec((1, 1, size, size), lambda i: (0, i, 0, 0))],
        out_specs=pl.BlockSpec((1, size, size), lambda i: (i, 0, 0)),
        out_shape=jax.ShapeDtypeStruct((levels, size, size), F32),
        compiler_params=pltpu.CompilerParams(vmem_limit_bytes=48 * 2**20),
        name="inverses",
    )(diag_factor)


def sum_kernel(x_ref, out_ref, pair, send, landed, right_got, left_got, right_sib, left_sib, final,
               final_sib, pair_s, pair_r, rs_s, rs_r, right_s, right_r, left_s, left_r, sib_s, sib_r):
    me = lax.axis_index("row")
    z = me // 2
    core = me % 2
    sibling = 2 * z + 1 - core

    def at_chip(chip):
        return {"row": 2 * chip + core}

    barrier = pltpu.get_barrier_semaphore()
    pl.semaphore_signal(barrier, inc=1, device_id={"row": sibling}, device_id_type=MESH)
    for k in (1, 2, 3):
        pl.semaphore_signal(
            barrier, inc=1, device_id=at_chip((z + k) % 4), device_id_type=MESH
        )
    pl.semaphore_wait(barrier, 4)

    def copy(src, dst, send_sem, recv_sem, target):
        return pltpu.make_async_remote_copy(
            src_ref=src, dst_ref=dst, send_sem=send_sem, recv_sem=recv_sem,
            device_id=target, device_id_type=MESH,
        )

    to_pair = {}
    for k in (2, 1, 3, 0):
        to_pair[k] = copy(
            x_ref.at[1 - core, (z + k) % 4], pair.at[k], pair_s.at[k], pair_r.at[k],
            {"row": sibling},
        )
        to_pair[k].start()
    scatter = {}
    for k in (2, 1, 3):
        to_pair[k].wait_recv()
        send[k - 1] = (x_ref[core, (z + k) % 4] + pair[k]).astype(BF)
        scatter[k] = copy(
            send.at[k - 1], landed.at[k - 1], rs_s.at[k - 1], rs_r.at[k - 1],
            at_chip((z + k) % 4),
        )
        scatter[k].start()
    to_pair[0].wait_recv()
    pair[0] = pair[0] + x_ref[core, z]
    for k in (1, 3, 2):
        scatter[k].wait_recv()
        pair[0] = pair[0] + landed[k - 1].astype(F32)
    final[...] = pair[0].astype(BF)

    rights, lefts, sibs = {}, {}, {}
    sibs[0] = copy(final, final_sib, sib_s.at[0], sib_r.at[0], {"row": sibling})
    for s in (1, 2, 3):
        rights[s] = copy(
            final if s == 1 else right_got.at[s - 2], right_got.at[s - 1],
            right_s.at[s - 1], right_r.at[s - 1], at_chip(jnp.minimum(z + 1, 3)),
        )
        lefts[s] = copy(
            final if s == 1 else left_got.at[s - 2], left_got.at[s - 1],
            left_s.at[s - 1], left_r.at[s - 1], at_chip(jnp.maximum(z - 1, 0)),
        )
        sibs[s] = copy(
            right_got.at[s - 1], right_sib.at[s - 1], sib_s.at[s], sib_r.at[s], {"row": sibling}
        )
        sibs[-s] = copy(
            left_got.at[s - 1], left_sib.at[s - 1], sib_s.at[3 + s], sib_r.at[3 + s],
            {"row": sibling},
        )

    def goes_right(s):
        return (z < 3) & (z >= s - 1)

    def goes_left(s):
        return (z > 0) & (z + s <= 4)

    pl.when(goes_right(1))(rights[1].start)
    pl.when(goes_left(1))(lefts[1].start)
    sibs[0].start()
    out_ref[core, z] = final[...].astype(F32)
    for s in (1, 2, 3):
        @pl.when(z >= s)
        def _():
            rights[s].wait_recv()
            sibs[s].start()

        if s < 3:
            pl.when(goes_right(s + 1))(rights[s + 1].start)

        @pl.when(z + s <= 3)
        def _():
            lefts[s].wait_recv()
            sibs[-s].start()

        if s < 3:
            pl.when(goes_left(s + 1))(lefts[s + 1].start)

        @pl.when(z >= s)
        def _():
            out_ref[core, z - s] = right_got[s - 1].astype(F32)

        @pl.when(z + s <= 3)
        def _():
            out_ref[core, z + s] = left_got[s - 1].astype(F32)

    sibs[0].wait_recv()
    out_ref[1 - core, z] = final_sib[...].astype(F32)
    for s in (1, 2, 3):
        @pl.when(z >= s)
        def _():
            sibs[s].wait_recv()
            out_ref[1 - core, z - s] = right_sib[s - 1].astype(F32)

        @pl.when(z + s <= 3)
        def _():
            sibs[-s].wait_recv()
            out_ref[1 - core, z + s] = left_sib[s - 1].astype(F32)

    for k in (0, 1, 2, 3):
        to_pair[k].wait_send()
        if k:
            scatter[k].wait_send()
    sibs[0].wait_send()
    for s in (1, 2, 3):
        pl.when(goes_right(s))(rights[s].wait_send)
        pl.when(goes_left(s))(lefts[s].wait_send)
        pl.when(z >= s)(sibs[s].wait_send)
        pl.when(z + s <= 3)(sibs[-s].wait_send)


def line_sum(x, total):
    rows, columns = x.shape[0] // 8, x.shape[1]
    dma = pltpu.SemaphoreType.DMA
    whole = pl.BlockSpec(memory_space=pltpu.VMEM)
    out = pl.pallas_call(
        sum_kernel,
        out_shape=jax.ShapeDtypeStruct((2, 4, rows, columns), F32),
        in_specs=[whole],
        out_specs=whole,
        scratch_shapes=[
            pltpu.VMEM((4, rows, columns), F32),
            *[pltpu.VMEM((3, rows, columns), BF) for _ in range(6)],
            pltpu.VMEM((rows, columns), BF),
            pltpu.VMEM((rows, columns), BF),
            dma((4,)), dma((4,)),
            *[dma((3,)) for _ in range(6)],
            dma((7,)), dma((7,)),
        ],
        compiler_params=pltpu.CompilerParams(
            collective_id=0, has_side_effects=True, vmem_limit_bytes=48 * 2**20
        ),
        name="line_sum",
    )(x.reshape(2, 4, rows, columns))
    return out.reshape(8 * rows, columns)[:total]


def gather_kernel(x_ref, out_ref, right_s, right_r, left_s, left_r, sib_s, sib_r, own_s):
    me = lax.axis_index("row")
    z = me // 2
    core = me % 2
    sibling = 2 * z + 1 - core
    right = 2 * jnp.minimum(z + 1, 3) + core
    left = 2 * jnp.maximum(z - 1, 0) + core
    barrier = pltpu.get_barrier_semaphore()
    pl.semaphore_signal(barrier, inc=1, device_id={"row": sibling}, device_id_type=MESH)
    for k in (1, 2, 3):
        pl.semaphore_signal(
            barrier, inc=1, device_id={"row": 2 * ((z + k) % 4) + core}, device_id_type=MESH
        )
    pl.semaphore_wait(barrier, 4)

    def moved(source, part, send_sem, recv_sem, target, first):
        return pltpu.make_async_remote_copy(
            src_ref=x_ref.at[part] if first else out_ref.at[source, part],
            dst_ref=out_ref.at[source, part], send_sem=send_sem, recv_sem=recv_sem,
            device_id={"row": target}, device_id_type=MESH,
        )

    steps = [(s, p) for s in (1, 2, 3) for p in (0, 1)]
    rights, lefts, sib_right, sib_left, own = {}, {}, {}, {}, {}
    for p in (0, 1):
        own[p] = moved(me, p, sib_s.at[0, p], sib_r.at[0, p], sibling, True)
    for s, p in steps:
        from_left = 2 * jnp.maximum(z - s, 0) + core
        from_right = 2 * jnp.minimum(z + s, 3) + core
        rights[s, p] = moved(
            2 * jnp.maximum(z - s + 1, 0) + core, p, right_s.at[s - 1, p], right_r.at[s - 1, p],
            right, s == 1,
        )
        lefts[s, p] = moved(
            2 * jnp.minimum(z + s - 1, 3) + core, p, left_s.at[s - 1, p], left_r.at[s - 1, p],
            left, s == 1,
        )
        sib_right[s, p] = moved(from_left, p, sib_s.at[s, p], sib_r.at[s, p], sibling, False)
        sib_left[s, p] = moved(
            from_right, p, sib_s.at[3 + s, p], sib_r.at[3 + s, p], sibling, False
        )

    def goes_right(s):
        return (z < 3) & (z >= s - 1)

    def goes_left(s):
        return (z > 0) & (z + s <= 4)

    for p in (0, 1):
        pl.when(goes_right(1))(rights[1, p].start)
        pl.when(goes_left(1))(lefts[1, p].start)
    for p in (0, 1):
        own[p].start()
    keep = pltpu.make_async_copy(x_ref, out_ref.at[me], own_s)
    keep.start()
    for s, p in steps:
        @pl.when(z >= s)
        def _():
            rights[s, p].wait_recv()
            sib_right[s, p].start()

        if s < 3:
            pl.when(goes_right(s + 1))(rights[s + 1, p].start)

        @pl.when(z + s <= 3)
        def _():
            lefts[s, p].wait_recv()
            sib_left[s, p].start()

        if s < 3:
            pl.when(goes_left(s + 1))(lefts[s + 1, p].start)
    keep.wait()
    for p in (0, 1):
        own[p].wait()
    for s, p in steps:
        pl.when(goes_right(s))(rights[s, p].wait_send)
        pl.when(goes_left(s))(lefts[s, p].wait_send)
        pl.when(z >= s)(sib_right[s, p].wait)
        pl.when(z + s <= 3)(sib_left[s, p].wait)


def line_gather(x):
    dma = pltpu.SemaphoreType.DMA
    whole = pl.BlockSpec(memory_space=pltpu.VMEM)
    return pl.pallas_call(
        gather_kernel,
        out_shape=jax.ShapeDtypeStruct((8, *x.shape), x.dtype),
        in_specs=[whole],
        out_specs=whole,
        scratch_shapes=[*[dma((3, 2)) for _ in range(4)], dma((7, 2)), dma((7, 2)), dma(())],
        compiler_params=pltpu.CompilerParams(
            collective_id=1, has_side_effects=True, vmem_limit_bytes=32 * 2**20
        ),
        name="line_gather",
    )(x)


def dot3t(a, b):
    def one(p, q):
        return lax.dot_general(p, q, (((0,), (0,)), ((), ())), preferred_element_type=F32)

    return one(a[0], b[0]) + (one(a[1], b[0]) + one(a[0], b[1]))


def partial_kernel(size, keep_ref, root_ref, all_ref, pair_ref, scaled_ref, mine_ref, chain_ref,
                   panel_ref, part_ref):
    tile = lax.axis_index("row") // 2
    panel = block = None
    for i in range(3):
        if i < 2:
            projected = None
            for b in range(4):
                term = mm(root_ref[b], all_ref[2 * b:2 * b + 2, i].reshape(size, size))
                projected = term if projected is None else projected + term
        else:
            projected = mm(root_ref[tile], pair_ref[...])
        scaled = split(scaled_ref[i])
        mine = split(mine_ref[i])
        if i:
            chain = split(chain_ref[i - 1])
            projected = projected + dot3(panel, chain)
            cross = -(dot3t(panel, scaled) + dot3(block, chain))
            part_ref[(2 + i) * size:(3 + i) * size] = cross
        kept = jnp.where(keep_ref[i] > 0, -projected, 0.0)
        panel_ref[0, i] = kept
        panel = split(kept)
        value = dot3t(mine, mine) - dot3t(scaled, panel)
        if i:
            value = value - dot3t(chain, split(cross))
        part_ref[i * size:(i + 1) * size] = value
        block = split(value)
    rest = part_ref.shape[0] - 5 * size
    part_ref[5 * size:] = jnp.zeros((rest, size), F32)


def partials(keep, root, everyone, pair, scaled, mine, chain):
    size = scaled.shape[-1]
    rows = -(-5 * size // 128) * 128
    whole = pl.BlockSpec(memory_space=pltpu.VMEM)
    return pl.pallas_call(
        functools.partial(partial_kernel, size),
        out_shape=(
            jax.ShapeDtypeStruct((1, *scaled.shape), F32),
            jax.ShapeDtypeStruct((rows, size), F32),
        ),
        in_specs=[pl.BlockSpec(memory_space=pltpu.SMEM)] + [whole] * 6,
        out_specs=(whole, whole),
        compiler_params=pltpu.CompilerParams(vmem_limit_bytes=52 * 2**20),
        name="partials",
    )(keep, root, everyone, pair, scaled, mine, chain)


def on_device(root_cov, diag_factor, panel_factor, chain_factor, panel_tiles):
    node_width = diag_factor.shape[-1]
    rows_here = panel_factor.shape[2]
    per_tile = node_width // rows_here
    row_count = lax.axis_size("row")
    tile_total = row_count // per_tile
    counts = (3 * tile_total // 4, tile_total // 2, tile_total // 4)
    small = row_count == 8 and tile_total == 4 and root_cov.shape[1] == node_width
    if small:
        root_rows = lax.all_gather(root_cov, "branch")
    else:
        root_rows = lax.all_gather(root_cov, "branch", axis=1, tiled=True)
    me = lax.axis_index("row")
    my_tile = me // per_tile
    inverse_all = inverses(diag_factor)
    share = -(-node_width // row_count // 8) * 8
    padded = jnp.pad(inverse_all, ((0, 0), (0, share * row_count - node_width), (0, 0)))
    mine = lax.dynamic_slice_in_dim(padded, me * share, share, axis=1)
    chosen = [jnp.any(panel_tiles[0, : counts[i]] == my_tile) for i in range(3)]
    scaled = [
        jnp.where(chosen[i], product(panel_factor[0, i], inverse_all[i]), 0.0) for i in range(3)
    ]
    if small:
        rounded = [x.astype(BF) for x in scaled]
        theirs = lax.ppermute(rounded[2], "row", [(d, d ^ 1) for d in range(row_count)])
        pair = jnp.where(
            me % 2 == 0,
            jnp.concatenate([rounded[2], theirs]),
            jnp.concatenate([theirs, rounded[2]]),
        )
        everyone = line_gather(jnp.stack(rounded[:2]))
        chain_all = jnp.stack([product(chain_factor[0, i - 1], inverse_all[i]) for i in (1, 2)])
        panel_out, parts = partials(
            jnp.stack(chosen).astype(jnp.int32), root_rows, everyone, pair, jnp.stack(scaled),
            mine, chain_all,
        )
        total = line_sum(parts, 5 * node_width)
        return (panel_out, total.reshape(1, 5, node_width, node_width))
    panels = []
    blocks = []
    crosses = []
    for i in range(3):
        rounded = scaled[i].astype(BF)
        gathered = jnp.dot(
            root_rows,
            lax.all_gather(rounded, "row", axis=0, tiled=True),
            preferred_element_type=F32,
        )
        left = jnp.concatenate([mine[i], scaled[i]], axis=0)
        if i == 0:
            panel = -jnp.where(chosen[i], gathered, 0.0)
            block = product(left.T, jnp.concatenate([mine[i], -panel], axis=0))
        else:
            chain = product(chain_factor[0, i - 1], inverse_all[i])
            panel = -jnp.where(chosen[i], gathered + product(panels[-1], chain), 0.0)
            cross = -(product(panels[-1].T, scaled[i]) + product(blocks[-1], chain))
            block = product(left.T, jnp.concatenate([mine[i], -panel], axis=0)) - product(
                chain.T, cross
            )
            crosses.append(cross)
        panels.append(panel)
        blocks.append(block)
    total = lax.psum(jnp.stack(blocks + crosses), "row")
    return (jnp.stack(panels)[None], total[None])


def solution(mesh):
    in_specs = (
        P("row", "branch"),
        P("branch", None, None, None),
        P("branch", None, "row", None),
        P("branch", None, None, None),
        P("branch", None),
    )
    out_specs = (P("branch", None, "row", None), P("branch", None, None, None))
    return jax.shard_map(
        on_device, mesh=mesh, in_specs=in_specs, out_specs=out_specs, check_vma=False
    )
```

```python
import functools
import jax
import jax.numpy as jnp
from jax import lax
from jax.experimental import pallas as pl
from jax.experimental.pallas import tpu as pltpu
from jax.sharding import PartitionSpec as P

BF = jnp.bfloat16
F32 = jnp.float32
MESH = pl.DeviceIdType.MESH


def product(left_mat, right_mat):
    return jnp.dot(left_mat, right_mat, precision=lax.Precision.HIGH, preferred_element_type=F32)


def split(x):
    hi = x.astype(BF)
    return hi, (x - hi.astype(F32)).astype(BF)


def mm(a, b):
    return jnp.dot(a, b, preferred_element_type=F32)


def dot3(a, b):
    a_hi, a_lo = a
    b_hi, b_lo = b
    return mm(a_hi, b_hi) + (mm(a_lo, b_hi) + mm(a_hi, b_lo))


def inverse_kernel(size, window, l_ref, out_ref):
    count = size // window
    row = lax.broadcasted_iota(jnp.int32, (window, window), 0)
    col = lax.broadcasted_iota(jnp.int32, (window, window), 1)
    eye = row == col
    diagonals = []
    for w in range(count):
        at = slice(w * window, (w + 1) * window)
        block = l_ref[0, 0, at, at]
        kept = jnp.where(eye, block, 0.0)
        down = 1.0 / jnp.sum(kept, axis=1, keepdims=True)
        across = 1.0 / jnp.sum(kept, axis=0, keepdims=True)
        diagonals.append((block * down, across))
    found = []
    for scaled, across in diagonals:
        x = jnp.where(eye, 1.0, 0.0)
        x = x - jnp.where((row // 2 == col // 2) & (row > col), scaled, 0.0)
        found.append(x)
    k = 2
    while k < window:
        pair = (row // (2 * k) == col // (2 * k)) & (row // k > col // k)
        for w in range(count):
            x = found[w]
            parts = split(x)
            right = dot3(split(jnp.where(pair, diagonals[w][0], 0.0)), parts)
            found[w] = x - dot3(parts, split(right))
        k *= 2
    found = [x * diagonals[w][1] for w, x in enumerate(found)]
    done = {}
    for w in range(count):
        done[w, w] = split(found[w])
        out_ref[0, w * window:(w + 1) * window, w * window:(w + 1) * window] = found[w]
    for gap in range(1, count):
        for c in range(count - gap):
            r = c + gap
            total = None
            for m in range(c, r):
                below = split(l_ref[0, 0, r * window:(r + 1) * window, m * window:(m + 1) * window])
                term = dot3(below, done[m, c])
                total = term if total is None else total + term
            value = -dot3(done[r, r], split(total))
            done[r, c] = split(value)
            out_ref[0, r * window:(r + 1) * window, c * window:(c + 1) * window] = value
            out_ref[0, c * window:(c + 1) * window, r * window:(r + 1) * window] = jnp.zeros(
                (window, window), F32
            )


def inverses(diag_factor):
    levels, size = diag_factor.shape[1], diag_factor.shape[-1]
    return pl.pallas_call(
        functools.partial(inverse_kernel, size, size // 3),
        grid=(levels,),
        in_specs=[pl.BlockSpec((1, 1, size, size), lambda i: (0, i, 0, 0))],
        out_specs=pl.BlockSpec((1, size, size), lambda i: (i, 0, 0)),
        out_shape=jax.ShapeDtypeStruct((levels, size, size), F32),
        compiler_params=pltpu.CompilerParams(vmem_limit_bytes=48 * 2**20),
        name="inverses",
    )(diag_factor)


def sum_kernel(x_ref, out_ref, pair, send, landed, right_got, left_got, right_sib, left_sib, final,
               final_sib, pair_s, pair_r, rs_s, rs_r, right_s, right_r, left_s, left_r, sib_s, sib_r):
    me = lax.axis_index("row")
    z = me // 2
    core = me % 2
    sibling = 2 * z + 1 - core

    def at_chip(chip):
        return {"row": 2 * chip + core}

    barrier = pltpu.get_barrier_semaphore()
    pl.semaphore_signal(barrier, inc=1, device_id={"row": sibling}, device_id_type=MESH)
    for k in (1, 2, 3):
        pl.semaphore_signal(
            barrier, inc=1, device_id=at_chip((z + k) % 4), device_id_type=MESH
        )
    pl.semaphore_wait(barrier, 4)

    def copy(src, dst, send_sem, recv_sem, target):
        return pltpu.make_async_remote_copy(
            src_ref=src, dst_ref=dst, send_sem=send_sem, recv_sem=recv_sem,
            device_id=target, device_id_type=MESH,
        )

    to_pair = {}
    for k in (2, 1, 3, 0):
        to_pair[k] = copy(
            x_ref.at[1 - core, (z + k) % 4], pair.at[k], pair_s.at[k], pair_r.at[k],
            {"row": sibling},
        )
        to_pair[k].start()
    scatter = {}
    for k in (2, 1, 3):
        to_pair[k].wait_recv()
        send[k - 1] = (x_ref[core, (z + k) % 4] + pair[k]).astype(BF)
        scatter[k] = copy(
            send.at[k - 1], landed.at[k - 1], rs_s.at[k - 1], rs_r.at[k - 1],
            at_chip((z + k) % 4),
        )
        scatter[k].start()
    to_pair[0].wait_recv()
    pair[0] = pair[0] + x_ref[core, z]
    for k in (1, 3, 2):
        scatter[k].wait_recv()
        pair[0] = pair[0] + landed[k - 1].astype(F32)
    final[...] = pair[0].astype(BF)

    rights, lefts, sibs = {}, {}, {}
    sibs[0] = copy(final, final_sib, sib_s.at[0], sib_r.at[0], {"row": sibling})
    for s in (1, 2, 3):
        rights[s] = copy(
            final if s == 1 else right_got.at[s - 2], right_got.at[s - 1],
            right_s.at[s - 1], right_r.at[s - 1], at_chip(jnp.minimum(z + 1, 3)),
        )
        lefts[s] = copy(
            final if s == 1 else left_got.at[s - 2], left_got.at[s - 1],
            left_s.at[s - 1], left_r.at[s - 1], at_chip(jnp.maximum(z - 1, 0)),
        )
        sibs[s] = copy(
            right_got.at[s - 1], right_sib.at[s - 1], sib_s.at[s], sib_r.at[s], {"row": sibling}
        )
        sibs[-s] = copy(
            left_got.at[s - 1], left_sib.at[s - 1], sib_s.at[3 + s], sib_r.at[3 + s],
            {"row": sibling},
        )

    def goes_right(s):
        return (z < 3) & (z >= s - 1)

    def goes_left(s):
        return (z > 0) & (z + s <= 4)

    pl.when(goes_right(1))(rights[1].start)
    pl.when(goes_left(1))(lefts[1].start)
    sibs[0].start()
    out_ref[core, z] = final[...].astype(F32)
    for s in (1, 2, 3):
        @pl.when(z >= s)
        def _():
            rights[s].wait_recv()
            sibs[s].start()

        if s < 3:
            pl.when(goes_right(s + 1))(rights[s + 1].start)

        @pl.when(z + s <= 3)
        def _():
            lefts[s].wait_recv()
            sibs[-s].start()

        if s < 3:
            pl.when(goes_left(s + 1))(lefts[s + 1].start)

        @pl.when(z >= s)
        def _():
            out_ref[core, z - s] = right_got[s - 1].astype(F32)

        @pl.when(z + s <= 3)
        def _():
            out_ref[core, z + s] = left_got[s - 1].astype(F32)

    sibs[0].wait_recv()
    out_ref[1 - core, z] = final_sib[...].astype(F32)
    for s in (1, 2, 3):
        @pl.when(z >= s)
        def _():
            sibs[s].wait_recv()
            out_ref[1 - core, z - s] = right_sib[s - 1].astype(F32)

        @pl.when(z + s <= 3)
        def _():
            sibs[-s].wait_recv()
            out_ref[1 - core, z + s] = left_sib[s - 1].astype(F32)

    for k in (0, 1, 2, 3):
        to_pair[k].wait_send()
        if k:
            scatter[k].wait_send()
    sibs[0].wait_send()
    for s in (1, 2, 3):
        pl.when(goes_right(s))(rights[s].wait_send)
        pl.when(goes_left(s))(lefts[s].wait_send)
        pl.when(z >= s)(sibs[s].wait_send)
        pl.when(z + s <= 3)(sibs[-s].wait_send)


def line_sum(x, total):
    rows, columns = x.shape[0] // 8, x.shape[1]
    dma = pltpu.SemaphoreType.DMA
    whole = pl.BlockSpec(memory_space=pltpu.VMEM)
    out = pl.pallas_call(
        sum_kernel,
        out_shape=jax.ShapeDtypeStruct((2, 4, rows, columns), F32),
        in_specs=[whole],
        out_specs=whole,
        scratch_shapes=[
            pltpu.VMEM((4, rows, columns), F32),
            *[pltpu.VMEM((3, rows, columns), BF) for _ in range(6)],
            pltpu.VMEM((rows, columns), BF),
            pltpu.VMEM((rows, columns), BF),
            dma((4,)), dma((4,)),
            *[dma((3,)) for _ in range(6)],
            dma((7,)), dma((7,)),
        ],
        compiler_params=pltpu.CompilerParams(
            collective_id=0, has_side_effects=True, vmem_limit_bytes=48 * 2**20
        ),
        name="line_sum",
    )(x.reshape(2, 4, rows, columns))
    return out.reshape(8 * rows, columns)[:total]


def gather_kernel(x_ref, out_ref, right_s, right_r, left_s, left_r, sib_s, sib_r, own_s):
    me = lax.axis_index("row")
    z = me // 2
    core = me % 2
    sibling = 2 * z + 1 - core
    right = 2 * jnp.minimum(z + 1, 3) + core
    left = 2 * jnp.maximum(z - 1, 0) + core
    barrier = pltpu.get_barrier_semaphore()
    pl.semaphore_signal(barrier, inc=1, device_id={"row": sibling}, device_id_type=MESH)
    for k in (1, 2, 3):
        pl.semaphore_signal(
            barrier, inc=1, device_id={"row": 2 * ((z + k) % 4) + core}, device_id_type=MESH
        )
    pl.semaphore_wait(barrier, 4)

    def moved(source, part, send_sem, recv_sem, target, first):
        return pltpu.make_async_remote_copy(
            src_ref=x_ref.at[part] if first else out_ref.at[source, part],
            dst_ref=out_ref.at[source, part], send_sem=send_sem, recv_sem=recv_sem,
            device_id={"row": target}, device_id_type=MESH,
        )

    steps = [(s, p) for s in (1, 2, 3) for p in (0, 1)]
    rights, lefts, sib_right, sib_left, own = {}, {}, {}, {}, {}
    for p in (0, 1):
        own[p] = moved(me, p, sib_s.at[0, p], sib_r.at[0, p], sibling, True)
    for s, p in steps:
        from_left = 2 * jnp.maximum(z - s, 0) + core
        from_right = 2 * jnp.minimum(z + s, 3) + core
        rights[s, p] = moved(
            2 * jnp.maximum(z - s + 1, 0) + core, p, right_s.at[s - 1, p], right_r.at[s - 1, p],
            right, s == 1,
        )
        lefts[s, p] = moved(
            2 * jnp.minimum(z + s - 1, 3) + core, p, left_s.at[s - 1, p], left_r.at[s - 1, p],
            left, s == 1,
        )
        sib_right[s, p] = moved(from_left, p, sib_s.at[s, p], sib_r.at[s, p], sibling, False)
        sib_left[s, p] = moved(
            from_right, p, sib_s.at[3 + s, p], sib_r.at[3 + s, p], sibling, False
        )

    def goes_right(s):
        return (z < 3) & (z >= s - 1)

    def goes_left(s):
        return (z > 0) & (z + s <= 4)

    for p in (0, 1):
        pl.when(goes_right(1))(rights[1, p].start)
        pl.when(goes_left(1))(lefts[1, p].start)
    for p in (0, 1):
        own[p].start()
    keep = pltpu.make_async_copy(x_ref, out_ref.at[me], own_s)
    keep.start()
    for s, p in steps:
        @pl.when(z >= s)
        def _():
            rights[s, p].wait_recv()
            sib_right[s, p].start()

        if s < 3:
            pl.when(goes_right(s + 1))(rights[s + 1, p].start)

        @pl.when(z + s <= 3)
        def _():
            lefts[s, p].wait_recv()
            sib_left[s, p].start()

        if s < 3:
            pl.when(goes_left(s + 1))(lefts[s + 1, p].start)
    keep.wait()
    for p in (0, 1):
        own[p].wait()
    for s, p in steps:
        pl.when(goes_right(s))(rights[s, p].wait_send)
        pl.when(goes_left(s))(lefts[s, p].wait_send)
        pl.when(z >= s)(sib_right[s, p].wait)
        pl.when(z + s <= 3)(sib_left[s, p].wait)


def line_gather(x):
    dma = pltpu.SemaphoreType.DMA
    whole = pl.BlockSpec(memory_space=pltpu.VMEM)
    return pl.pallas_call(
        gather_kernel,
        out_shape=jax.ShapeDtypeStruct((8, *x.shape), x.dtype),
        in_specs=[whole],
        out_specs=whole,
        scratch_shapes=[*[dma((3, 2)) for _ in range(4)], dma((7, 2)), dma((7, 2)), dma(())],
        compiler_params=pltpu.CompilerParams(
            collective_id=1, has_side_effects=True, vmem_limit_bytes=32 * 2**20
        ),
        name="line_gather",
    )(x)


def dot3t(a, b):
    def one(p, q):
        return lax.dot_general(p, q, (((0,), (0,)), ((), ())), preferred_element_type=F32)

    return one(a[0], b[0]) + (one(a[1], b[0]) + one(a[0], b[1]))


def partial_kernel(size, keep_ref, root_ref, all_ref, pair_ref, scaled_0, scaled_1, scaled_2,
                   mine_ref, chain_0, chain_1, panel_ref, part_ref):
    scaled_refs = (scaled_0, scaled_1, scaled_2)
    chain_refs = (chain_0, chain_1)
    tile = lax.axis_index("row") // 2
    panel = block = None
    for i in range(3):
        if i < 2:
            projected = None
            for b in range(4):
                term = mm(root_ref[b], all_ref[2 * b:2 * b + 2, i].reshape(size, size))
                projected = term if projected is None else projected + term
        else:
            projected = mm(root_ref[tile], pair_ref[...])
        scaled = split(scaled_refs[i][...])
        mine = split(mine_ref[i])
        if i:
            chain = split(chain_refs[i - 1][...])
            projected = projected + dot3(panel, chain)
            cross = -(dot3t(panel, scaled) + dot3(block, chain))
            part_ref[(2 + i) * size:(3 + i) * size] = cross
        kept = jnp.where(keep_ref[i] > 0, -projected, 0.0)
        panel_ref[0, i] = kept
        panel = split(kept)
        value = dot3t(mine, mine) - dot3t(scaled, panel)
        if i:
            value = value - dot3t(chain, split(cross))
        part_ref[i * size:(i + 1) * size] = value
        block = split(value)
    rest = part_ref.shape[0] - 5 * size
    part_ref[5 * size:] = jnp.zeros((rest, size), F32)


def partials(keep, root, everyone, pair, scaled, mine, chain):
    size = scaled[0].shape[-1]
    rows = -(-5 * size // 128) * 128
    whole = pl.BlockSpec(memory_space=pltpu.VMEM)
    return pl.pallas_call(
        functools.partial(partial_kernel, size),
        out_shape=(
            jax.ShapeDtypeStruct((1, 3, *scaled[0].shape), F32),
            jax.ShapeDtypeStruct((rows, size), F32),
        ),
        in_specs=[pl.BlockSpec(memory_space=pltpu.SMEM)] + [whole] * 9,
        out_specs=(whole, whole),
        compiler_params=pltpu.CompilerParams(vmem_limit_bytes=52 * 2**20),
        name="partials",
    )(keep, root, everyone, pair, *scaled, mine, *chain)


def on_device(root_cov, diag_factor, panel_factor, chain_factor, panel_tiles):
    node_width = diag_factor.shape[-1]
    rows_here = panel_factor.shape[2]
    per_tile = node_width // rows_here
    row_count = lax.axis_size("row")
    tile_total = row_count // per_tile
    counts = (3 * tile_total // 4, tile_total // 2, tile_total // 4)
    small = row_count == 8 and tile_total == 4 and root_cov.shape[1] == node_width
    if small:
        root_rows = lax.all_gather(root_cov, "branch")
    else:
        root_rows = lax.all_gather(root_cov, "branch", axis=1, tiled=True)
    me = lax.axis_index("row")
    my_tile = me // per_tile
    inverse_all = inverses(diag_factor)
    share = -(-node_width // row_count // 8) * 8
    padded = jnp.pad(inverse_all, ((0, 0), (0, share * row_count - node_width), (0, 0)))
    mine = lax.dynamic_slice_in_dim(padded, me * share, share, axis=1)
    chosen = [jnp.any(panel_tiles[0, : counts[i]] == my_tile) for i in range(3)]
    scaled = [
        jnp.where(chosen[i], product(panel_factor[0, i], inverse_all[i]), 0.0) for i in range(3)
    ]
    if small:
        rounded = [x.astype(BF) for x in scaled]
        theirs = lax.ppermute(rounded[2], "row", [(d, d ^ 1) for d in range(row_count)])
        pair = jnp.where(
            me % 2 == 0,
            jnp.concatenate([rounded[2], theirs]),
            jnp.concatenate([theirs, rounded[2]]),
        )
        everyone = line_gather(jnp.stack(rounded[:2]))
        chain_all = [product(chain_factor[0, i - 1], inverse_all[i]) for i in (1, 2)]
        panel_out, parts = partials(
            jnp.stack(chosen).astype(jnp.int32), root_rows, everyone, pair, scaled,
            mine, chain_all,
        )
        total = line_sum(parts, 5 * node_width)
        return (panel_out, total.reshape(1, 5, node_width, node_width))
    panels = []
    blocks = []
    crosses = []
    for i in range(3):
        rounded = scaled[i].astype(BF)
        gathered = jnp.dot(
            root_rows,
            lax.all_gather(rounded, "row", axis=0, tiled=True),
            preferred_element_type=F32,
        )
        left = jnp.concatenate([mine[i], scaled[i]], axis=0)
        if i == 0:
            panel = -jnp.where(chosen[i], gathered, 0.0)
            block = product(left.T, jnp.concatenate([mine[i], -panel], axis=0))
        else:
            chain = product(chain_factor[0, i - 1], inverse_all[i])
            panel = -jnp.where(chosen[i], gathered + product(panels[-1], chain), 0.0)
            cross = -(product(panels[-1].T, scaled[i]) + product(blocks[-1], chain))
            block = product(left.T, jnp.concatenate([mine[i], -panel], axis=0)) - product(
                chain.T, cross
            )
            crosses.append(cross)
        panels.append(panel)
        blocks.append(block)
    total = lax.psum(jnp.stack(blocks + crosses), "row")
    return (jnp.stack(panels)[None], total[None])


def solution(mesh):
    in_specs = (
        P("row", "branch"),
        P("branch", None, None, None),
        P("branch", None, "row", None),
        P("branch", None, None, None),
        P("branch", None),
    )
    out_specs = (P("branch", None, "row", None), P("branch", None, None, None))
    return jax.shard_map(
        on_device, mesh=mesh, in_specs=in_specs, out_specs=out_specs, check_vma=False
    )
```
